32 devices in a mesh: ctx: 8 (over z, y), head: 4 (over x, core).
Axes of the slice: x: 2, y: 2, z: 4, core: 2. Of those that a mesh axis runs over, the one named last changes fastest.
Arguments:
- queries: bfloat16 [2048, 2048], P('ctx', 'head'), may hold values from -34 to 34
- keys: bfloat16 [2048, 2048], P('ctx', 'head'), may hold values from -34 to 34
- values: bfloat16 [2048, 2048], P('ctx', 'head'), may hold values from -6 to 6
- output_grad: bfloat16 [2048, 4096], P('ctx', 'head'), may hold values from -6 to 6
- out_weight: bfloat16 [2048, 4096], P('head'), may hold values from -0.125 to 0.125
- random_blocks: int32 [16, 32, 3], replicated, may hold values from 0 to 31, as said below
- global_blocks: int32 [2], replicated, may hold values from 0 to 31, as said below
Outputs:
- output: bfloat16 [2048, 4096], P('ctx', 'head')
- query_grad: bfloat16 [2048, 2048], P('ctx', 'head')
- key_grad: bfloat16 [2048, 2048], P('ctx', 'head')
- value_grad: bfloat16 [2048, 2048], P('ctx', 'head')
The draws below stay inside these ranges and needn't reach their ends.
Inputs may be any that keep to these rules, and one draw needn't show every extreme that they name: Every entry random_blocks[h, i, r] names a block j with j // 4 != i // 4. For each group of 4 heads (heads g * 4 to (g + 1) * 4 - 1) and each aligned run of 4 query blocks, the 48 entries name blocks of any one other run at most 7 times, and of some run exactly 7 times. `global_blocks`: the 2 entries are distinct, and one of them is the last block.
All inputs are finite; a program needn't handle non-finite values.
Results may differ from the reference program's by a relative error of at most 0.027.
Values may be sent and summed in bfloat16 or wider, within the bound.
A program may use at most 128 MiB of HBM per device.

```python
import jax
import jax.numpy as jnp
from jax import lax

D = 4096
H = 16
HD = 128
BLK = 64
R = 3
G = 2
NB = 4
HL = 4
NBLK = 32
TOKENS = 2048


def paired_fields(key):
    seeded = jax.random.fold_in(key, 11)
    first_key, second_key = jax.random.split(seeded, 2)
    field_shape = (TOKENS, H * HD)
    query_field = jax.random.truncated_normal(first_key, -6.0, 6.0, field_shape, jnp.float32)
    key_field = jax.random.truncated_normal(second_key, -6.0, 6.0, field_shape, jnp.float32)
    return (query_field, key_field)


def draw_queries(key, part):
    query_field, key_field = paired_fields(key)
    return query_field.astype(jnp.bfloat16)


def draw_keys(key, part):
    query_field, key_field = paired_fields(key)
    return key_field.astype(jnp.bfloat16)


def draw_random_blocks(key, part):
    shards = NBLK // NB
    groups = H // HL
    requests = HL * NB * R
    seeded = jax.random.fold_in(key, 23)

    def per_unit(unit_key):
        first_key, second_key, third_key = jax.random.split(unit_key, 3)
        stepping = jax.random.permutation(first_key, shards - 1) + 1
        cyclic = stepping[jnp.arange(requests) % (shards - 1)]
        cyclic = cyclic[jax.random.permutation(second_key, requests)]
        within = jax.random.randint(third_key, (requests,), 0, NB)
        return (cyclic, within)
    unit_keys = jax.random.split(seeded, groups * shards)
    offsets, within = jax.vmap(per_unit)(unit_keys)
    offsets = offsets.reshape(groups, shards, HL, NB, R)
    within = within.reshape(groups, shards, HL, NB, R)
    shard_ids = jnp.arange(shards).reshape(1, shards, 1, 1, 1)
    owners = (shard_ids + offsets) % shards
    named = owners * NB + within
    return named.transpose(0, 2, 1, 3, 4).reshape(H, NBLK, R).astype(jnp.int32)


def draw_global_blocks(key, part):
    seeded = jax.random.fold_in(key, 37)
    first_key, second_key = jax.random.split(seeded, 2)
    others = jax.random.permutation(first_key, NBLK - 1)[:G - 1].astype(jnp.int32)
    listed = jnp.concatenate([jnp.full((1,), NBLK - 1, dtype=jnp.int32), others])
    turning = jax.random.randint(second_key, (), 0, G)
    return jnp.roll(listed, turning).astype(jnp.int32)


def levels(key, shape, pieces, low, high):
    factor_of, own = 1.0, jax.random.fold_in(key, 6)
    for dim, parts in pieces:
        steps = jnp.exp(jax.random.uniform(jax.random.fold_in(own, dim), (parts,), jnp.float32, low / len(pieces), high / len(pieces)))
        factor_of = factor_of * jnp.repeat(steps, shape[dim] // parts).reshape([-1 if axis == dim else 1 for axis in range(len(shape))])
    return factor_of


def scatter_about(own_key, dims, deviation, most, cuts=(), held_as=jnp.bfloat16):
    drawn = deviation * jax.random.normal(own_key, dims, jnp.float32)
    if cuts:
        drawn = drawn * levels(own_key, dims, cuts, -0.22, 0.18)
    return jnp.clip(drawn, -most, most).astype(held_as)


def setup_inputs(seed: int = 0) -> dict:
    key_of = jax.random.split(jax.random.key(seed), 8)
    return {
        "queries": draw_queries(jax.random.fold_in(key_of[7], 71), 0),
        "keys": draw_keys(jax.random.fold_in(key_of[7], 71), 0),
        "values": scatter_about(key_of[2], (TOKENS, H * HD), 1.0, 6.0, ((0, 8), (1, 4))),
        "output_grad": scatter_about(key_of[3], (TOKENS, D), 1.0, 6.0, ((0, 8), (1, 4))),
        "out_weight": scatter_about(key_of[4], (H * HD, D), (H * HD) ** -0.5, 0.125, ((0, 4),)),
        "random_blocks": draw_random_blocks(jax.random.fold_in(key_of[7], 71), 0),
        "global_blocks": draw_global_blocks(jax.random.fold_in(key_of[7], 71), 0),
    }


def rounded(field_in):
    return lax.optimization_barrier(field_in.astype(jnp.bfloat16)).astype(jnp.float32)


def key_lists(head_random, global_blocks):
    block_count = head_random.shape[0]
    block_ids = jnp.arange(block_count, dtype=jnp.int32)
    window = block_ids[:, None] + jnp.arange(3, dtype=jnp.int32)[None, :] - 1
    inside = (window >= 0) & (window < block_count)
    window = jnp.clip(window, 0, block_count - 1).astype(jnp.int32)
    global_rows = jnp.broadcast_to(global_blocks[None, :], (block_count, G)).astype(jnp.int32)
    listing = jnp.concatenate([window, global_rows, head_random.astype(jnp.int32)], axis=1)
    alive_mask = jnp.concatenate([inside, jnp.ones((block_count, G + R), dtype=bool)], axis=1)
    return listing, alive_mask


def logits_of(query_head, key_tiles, alive_mask):
    scaling = HD ** -0.5
    logits = jnp.einsum("nqd,nkbd->nqkb", query_head.astype(jnp.float32), key_tiles.astype(jnp.float32)) * scaling
    return jnp.where(alive_mask[:, None, :, None], logits, -jnp.inf)


def forward_head(operands):
    query_head, key_head, value_head, listing, alive_mask = operands
    key_tiles = key_head[listing]
    value_tiles = value_head[listing]
    logits = logits_of(query_head, key_tiles, alive_mask)
    row_max = jnp.max(logits, axis=(2, 3))
    log_total = row_max + jnp.log(jnp.sum(jnp.exp(logits - row_max[:, :, None, None]), axis=(2, 3)))
    weights_low = rounded(jnp.exp(logits - log_total[:, :, None, None]))
    attended = jnp.einsum("nqkb,nkbd->nqd", weights_low, value_tiles.astype(jnp.float32))
    return attended.astype(jnp.bfloat16), log_total


def backward_head(operands):
    query_head, key_head, value_head, attended, grad_head, log_total, listing, alive_mask = operands
    key_tiles = key_head[listing]
    value_tiles = value_head[listing]
    logits = logits_of(query_head, key_tiles, alive_mask)
    weights = jnp.exp(logits - log_total[:, :, None, None])
    weights_low = rounded(weights)
    grad_wide = grad_head.astype(jnp.float32)
    delta_rows = jnp.sum(grad_wide * attended.astype(jnp.float32), axis=2)
    products = jnp.einsum("nqd,nkbd->nqkb", grad_wide, value_tiles.astype(jnp.float32))
    logit_grad = rounded(weights * (products - delta_rows[:, :, None, None]))
    scaling = HD ** -0.5
    query_grad = jnp.einsum("nqkb,nkbd->nqd", logit_grad, key_tiles.astype(jnp.float32)) * scaling
    key_part = jnp.einsum("nqkb,nqd->nkbd", logit_grad, query_head.astype(jnp.float32)) * scaling
    value_part = jnp.einsum("nqkb,nqd->nkbd", weights_low, grad_wide)
    fixed_count = 3 + G
    key_part = jnp.concatenate([key_part[:, :fixed_count], rounded(key_part[:, fixed_count:])], axis=1)
    value_part = jnp.concatenate([value_part[:, :fixed_count], rounded(value_part[:, fixed_count:])], axis=1)
    zero_tiles = jnp.zeros(key_head.shape, jnp.float32)
    key_grad = zero_tiles.at[listing].add(key_part)
    value_grad = zero_tiles.at[listing].add(value_part)
    return query_grad.astype(jnp.bfloat16), key_grad.astype(jnp.bfloat16), value_grad.astype(jnp.bfloat16)


def reference(queries, keys, values, output_grad, out_weight, random_blocks, global_blocks):
    def by_head(field):
        return field.reshape(NBLK, BLK, H, HD).transpose(2, 0, 1, 3)

    def back_rows(field):
        return field.transpose(1, 2, 0, 3).reshape(TOKENS, H * HD)

    listings, alive_masks = jax.vmap(lambda head_table: key_lists(head_table, global_blocks))(random_blocks)
    query_heads = by_head(queries)
    key_heads = by_head(keys)
    value_heads = by_head(values)
    attended, log_totals = lax.map(forward_head, (query_heads, key_heads, value_heads, listings, alive_masks))
    flat = back_rows(attended)
    output = jnp.dot(flat.astype(jnp.float32), out_weight.astype(jnp.float32), preferred_element_type=jnp.float32).astype(jnp.bfloat16)
    attn_grad = jnp.dot(output_grad.astype(jnp.float32), out_weight.astype(jnp.float32).T, preferred_element_type=jnp.float32).astype(jnp.bfloat16)
    query_grad, key_grad, value_grad = lax.map(backward_head, (query_heads, key_heads, value_heads, attended, by_head(attn_grad), log_totals, listings, alive_masks))
    return output, back_rows(query_grad), back_rows(key_grad), back_rows(value_grad)
```

```python
import functools

import jax
import jax.numpy as jnp
from jax import lax
from jax.experimental import pallas as pl
from jax.experimental.pallas import tpu as pltpu
from jax.sharding import PartitionSpec as P

HD = 128
BLK = 64
R = 3
G = 2


def with_halo(cells, sides, width):
    for axis, dim in sides:
        count = lax.axis_size(axis)
        ends = count - 1
        head = lax.slice_in_dim(cells, 0, width, axis=dim)
        tail = lax.slice_in_dim(cells, cells.shape[dim] - width, cells.shape[dim], axis=dim)
        cells = jnp.concatenate(
            [
                lax.ppermute(tail, axis, [(i, (i + 1) % count) for i in range(ends)]),
                cells,
                lax.ppermute(head, axis, [((i + 1) % count, i) for i in range(ends)]),
            ],
            axis=dim,
        )
    return cells


def send_plan(request_table, shards, blocks, my_shard):
    requests = request_table.shape[1]
    owners = request_table // blocks
    within = request_table % blocks
    request_ids = jnp.arange(requests, dtype=jnp.int32)
    earlier = (owners[:, :, None] == owners[:, None, :]) & (
        request_ids[None, None, :] < request_ids[None, :, None]
    )
    ranking = jnp.sum(earlier.astype(jnp.int32), axis=2)
    capacity = (requests + shards - 2) // (shards - 1)
    slot_ids = jnp.arange(capacity, dtype=jnp.int32)
    owned = (owners == my_shard)[:, None, :] & (ranking[:, None, :] == slot_ids[None, :, None])
    tile_ids = (request_ids // (blocks * R))[None, :] * blocks + within
    send_tiles = jnp.sum(jnp.where(owned, tile_ids[:, None, :], 0), axis=2).reshape(-1)
    send_alive = jnp.any(owned, axis=2).reshape(-1)
    my_owners = lax.dynamic_index_in_dim(owners, my_shard, 0, keepdims=False)
    my_ranks = lax.dynamic_index_in_dim(ranking, my_shard, 0, keepdims=False)
    return (send_tiles, send_alive, my_owners * capacity + my_ranks)


def pick_tiles(pair_tiles, send_tiles, blocks):
    return pair_tiles[send_tiles % blocks, :, send_tiles // blocks, :]


def pair_products(row_tiles, window, global_pairs, fetched, low_edge, high_edge):
    nearby = jnp.einsum(
        "nqhd,nwbhd->nhqwb",
        row_tiles,
        window[..., low_edge:high_edge],
        preferred_element_type=jnp.float32,
    )
    distant = jnp.einsum(
        "nqhd,gbhd->nhqgb",
        row_tiles,
        global_pairs[..., low_edge:high_edge],
        preferred_element_type=jnp.float32,
    )
    chance = jnp.einsum(
        "nqhd,hnrbd->nhqrb",
        row_tiles,
        fetched[..., low_edge:high_edge],
        preferred_element_type=jnp.float32,
    )
    return jnp.concatenate([nearby, distant, chance], axis=3)


def collect_rows(mixing, window, global_pairs, fetched, low_edge, high_edge):
    nearby = jnp.einsum(
        "nhqwb,nwbhd->nqhd",
        mixing[:, :, :, :3],
        window[..., low_edge:high_edge],
        preferred_element_type=jnp.float32,
    )
    distant = jnp.einsum(
        "nhqgb,gbhd->nqhd",
        mixing[:, :, :, 3 : 3 + G],
        global_pairs[..., low_edge:high_edge],
        preferred_element_type=jnp.float32,
    )
    chance = jnp.einsum(
        "nhqrb,hnrbd->nqhd",
        mixing[:, :, :, 3 + G :],
        fetched[..., low_edge:high_edge],
        preferred_element_type=jnp.float32,
    )
    return nearby + distant + chance


def tile_terms(mixing, row_tiles):
    nearby = jnp.einsum(
        "nhqwb,nqhd->nwbhd", mixing[:, :, :, :3], row_tiles, preferred_element_type=jnp.float32
    )
    distant = jnp.einsum(
        "nhqgb,nqhd->gbhd",
        mixing[:, :, :, 3 : 3 + G],
        row_tiles,
        preferred_element_type=jnp.float32,
    )
    chance = jnp.einsum(
        "nhqrb,nqhd->hnrbd", mixing[:, :, :, 3 + G :], row_tiles, preferred_element_type=jnp.float32
    )
    return (nearby, distant, chance)


def body(queries, keys, values, output_grad, out_weight, random_blocks, global_blocks):
    shards = lax.axis_size("ctx")
    my_shard = lax.axis_index("ctx")
    head_group = lax.axis_index("head")
    tok_local, width_local = queries.shape
    head_dim = HD
    heads_local = width_local // head_dim
    blocks = tok_local // BLK
    scaling = head_dim ** (-0.5)
    query_tiles = queries.reshape(blocks, BLK, heads_local, head_dim)
    pair_tiles = jnp.concatenate(
        [
            keys.reshape(blocks, BLK, heads_local, head_dim),
            values.reshape(blocks, BLK, heads_local, head_dim),
        ],
        axis=3,
    )
    head_table = lax.dynamic_slice_in_dim(random_blocks, head_group * heads_local, heads_local, 0)
    request_table = (
        head_table.reshape(heads_local, shards, blocks, R)
        .transpose(1, 0, 2, 3)
        .reshape(shards, heads_local * blocks * R)
    )
    send_tiles, send_alive, receive_rows = send_plan(request_table, shards, blocks, my_shard)
    received = lax.all_to_all(
        pick_tiles(pair_tiles, send_tiles, blocks), "ctx", split_axis=0, concat_axis=0, tiled=True
    )
    fetched = received[receive_rows].reshape(heads_local, blocks, R, BLK, 2 * head_dim)
    padded = with_halo(pair_tiles.reshape(tok_local, 2 * width_local), (("ctx", 0),), BLK)
    padded = padded.reshape(blocks + 2, BLK, heads_local, 2 * head_dim)
    window = jnp.stack([padded[offset : offset + blocks] for offset in range(3)], axis=1)
    global_owner = global_blocks // blocks
    global_local = global_blocks % blocks
    picked = pair_tiles[global_local]
    holding = jnp.where(
        (global_owner == my_shard)[:, None, None, None], picked.astype(jnp.float32), 0.0
    )
    global_pairs = lax.psum(holding, "ctx").astype(jnp.bfloat16)
    first_block = my_shard * blocks
    window_ids = first_block + jnp.arange(blocks)[:, None] + jnp.arange(3)[None, :] - 1
    inside = (window_ids >= 0) & (window_ids < blocks * shards)
    alive_mask = jnp.concatenate([inside, jnp.ones((blocks, G + R), dtype=bool)], axis=1)[
        :, None, None, :, None
    ]
    logits = jnp.where(
        alive_mask,
        pair_products(query_tiles, window, global_pairs, fetched, 0, head_dim) * scaling,
        -jnp.inf,
    )
    row_max = jnp.max(logits, axis=(3, 4))
    log_total = row_max + jnp.log(jnp.sum(jnp.exp(logits - row_max[..., None, None]), axis=(3, 4)))
    weights_full = jnp.exp(logits - log_total[..., None, None])
    weights_low = weights_full.astype(jnp.bfloat16)
    attended = collect_rows(
        weights_low, window, global_pairs, fetched, head_dim, 2 * head_dim
    ).astype(jnp.bfloat16)
    attended_flat = attended.reshape(tok_local, width_local)
    partial_value = jnp.dot(attended_flat, out_weight, preferred_element_type=jnp.float32)
    output = lax.psum_scatter(partial_value, "head", scatter_dimension=1, tiled=True).astype(
        jnp.bfloat16
    )
    grad_sum = lax.dot_general(
        lax.all_gather(output_grad, "head", axis=1, tiled=True),
        out_weight,
        (((1,), (1,)), ((), ())),
        preferred_element_type=jnp.float32,
    )
    grad_tiles = grad_sum.astype(jnp.bfloat16).reshape(blocks, BLK, heads_local, head_dim)
    delta_rows = jnp.sum(
        grad_tiles.astype(jnp.float32) * attended.astype(jnp.float32), axis=3
    ).transpose(0, 2, 1)
    products = pair_products(grad_tiles, window, global_pairs, fetched, head_dim, 2 * head_dim)
    logit_grad = (weights_full * (products - delta_rows[..., None, None])).astype(jnp.bfloat16)
    query_grad = (
        (collect_rows(logit_grad, window, global_pairs, fetched, 0, head_dim) * scaling)
        .astype(jnp.bfloat16)
        .reshape(tok_local, width_local)
    )
    key_nearby, key_distant, key_chance = tile_terms(logit_grad, query_tiles)
    value_nearby, value_distant, value_chance = tile_terms(weights_low, grad_tiles)
    nearby_terms = jnp.concatenate([key_nearby * scaling, value_nearby], axis=4)
    framed = sum(
        (
            jnp.pad(nearby_terms[:, offset], ((offset, 2 - offset), (0, 0), (0, 0), (0, 0)))
            for offset in range(3)
        )
    )
    edge_rows = jnp.concatenate([framed[0], framed[blocks + 1]], axis=0).reshape(
        2 * BLK, 2 * width_local
    )
    arrived = with_halo(edge_rows.astype(jnp.bfloat16), (("ctx", 0),), BLK).astype(edge_rows.dtype)
    local_grad = framed[1 : blocks + 1]
    local_grad = local_grad.at[0].add(arrived[:BLK].reshape(BLK, heads_local, 2 * head_dim))
    local_grad = local_grad.at[blocks - 1].add(
        arrived[3 * BLK :].reshape(BLK, heads_local, 2 * head_dim)
    )
    distant_terms = jnp.concatenate([key_distant * scaling, value_distant], axis=3)
    summed = lax.psum(distant_terms, "ctx")
    selector = (
        (global_owner == my_shard)[:, None] & (global_local[:, None] == jnp.arange(blocks)[None, :])
    ).astype(jnp.float32)
    local_grad = local_grad + jnp.einsum(
        "gn,gbhd->nbhd", selector, summed, precision=lax.Precision.HIGHEST
    )
    chance_terms = (
        jnp.concatenate([key_chance * scaling, value_chance], axis=4)
        .astype(jnp.bfloat16)
        .reshape(-1, BLK, 2 * head_dim)
    )
    outgoing_grads = (
        jnp.zeros((send_tiles.shape[0], BLK, 2 * head_dim), jnp.bfloat16)
        .at[receive_rows]
        .set(chance_terms)
    )
    returned = lax.all_to_all(outgoing_grads, "ctx", split_axis=0, concat_axis=0, tiled=True)
    segment_ids = jnp.where(send_alive, send_tiles, heads_local * blocks)
    gathered = jax.ops.segment_sum(
        returned.astype(jnp.float32), segment_ids, num_segments=heads_local * blocks + 1
    )[: heads_local * blocks]
    local_grad = local_grad + gathered.reshape(heads_local, blocks, BLK, 2 * head_dim).transpose(
        1, 2, 0, 3
    )
    key_grad = local_grad[..., :head_dim].astype(jnp.bfloat16).reshape(tok_local, width_local)
    value_grad = local_grad[..., head_dim:].astype(jnp.bfloat16).reshape(tok_local, width_local)
    return (output, query_grad, key_grad, value_grad)


MESH = pl.DeviceIdType.MESH
YN = 2
ZN = 4
HN = 4
PARTS = ((0, 48, True), (48, 160, False), (160, 256, False))
NP = len(PARTS)


def greet(z, y, head):
    bar = pltpu.get_barrier_semaphore()

    def hello(target):
        pl.semaphore_signal(bar, inc=1, device_id=target, device_id_type=MESH)

    hello({"ctx": z * YN + (1 - y)})
    for d in range(1, HN):
        hello({"head": lax.rem(head + d, HN)})

    @pl.when(z > 0)
    def _():
        hello({"ctx": (z - 1) * YN + y})

    @pl.when(z < ZN - 1)
    def _():
        hello({"ctx": (z + 1) * YN + y})

    lower = jnp.where(z > 0, 1, 0)
    upper = jnp.where(z < ZN - 1, 1, 0)
    pl.semaphore_wait(bar, HN + lower + upper)


def gather_kernel(k_ref, v_ref, og_ref, w_hbm, kv_ref, do_ref, ogbuf, wbuf, acc, wsem, ssem, rsem, hs, hr):
    me = lax.axis_index("ctx")
    head = lax.axis_index("head")
    z, y = me // YN, lax.rem(me, YN)
    width = k_ref.shape[1]
    cols = og_ref.shape[1]
    wcopy = pltpu.make_async_copy(w_hbm, wbuf, wsem)
    wcopy.start()
    kv_ref[me, :, :width] = k_ref[...]
    kv_ref[me, :, width:] = v_ref[...]
    greet(z, y, head)

    def copy(way, slot, p):
        lo, hi, _ = PARTS[p]
        at = kv_ref.at[slot, pl.ds(lo, hi - lo)]
        target = (z + 1) * YN + y if way == 0 else (z - 1) * YN + y if way == 1 else z * YN + (1 - y)
        return pltpu.make_async_remote_copy(
            src_ref=at,
            dst_ref=at,
            send_sem=ssem.at[(way * 8 + slot) * NP + p],
            recv_sem=rsem.at[slot * NP + p],
            device_id={"ctx": target},
            device_id_type=MESH,
        )

    def onward(way, slot, p, act):
        inside = z < ZN - 1 if way == 0 else z > 0

        @pl.when(inside)
        def _():
            act(copy(way, slot, p))

    def run(act, waiting):
        for p in range(NP):
            act(copy(2, me, p))
            onward(0, me, p, act)
            onward(1, me, p, act)
        if not waiting:
            send_heads()
            multiply(0)
        other = z * YN + (1 - y)
        for p in range(NP):
            if PARTS[p][2]:
                if not waiting:
                    copy(2, other, p).wait_recv()
                onward(0, other, p, act)
                onward(1, other, p, act)
        for t in range(1, ZN):
            for p in range(NP):
                for way in range(2):
                    zs = z - t if way == 0 else z + t

                    @pl.when((zs >= 0) & (zs < ZN))
                    def _():
                        slot = zs * YN + y
                        if not waiting:
                            copy(2, slot, p).wait_recv()
                        onward(way, slot, p, act)
                        if PARTS[p][2]:
                            over = zs * YN + (1 - y)
                            if not waiting:
                                copy(2, over, p).wait_recv()
                            onward(way, over, p, act)
                        else:
                            act(copy(2, slot, p))
            if not waiting:
                multiply(t)
        if not waiting:
            for zs in range(ZN):
                for p in range(NP):
                    if not PARTS[p][2]:
                        copy(2, zs * YN + (1 - y), p).wait_recv()

    order = (0, 1, 2, 3)

    def head_copy(d):
        return pltpu.make_async_remote_copy(
            src_ref=og_ref,
            dst_ref=ogbuf.at[d - 1],
            send_sem=hs.at[d - 1],
            recv_sem=hr.at[d - 1],
            device_id={"head": lax.rem(head + d, HN)},
            device_id_type=MESH,
        )

    def send_heads():
        for d in range(1, HN):
            head_copy(d).start()
        wcopy.wait()

    def multiply(d):
        source = lax.rem(head - order[d] + HN, HN)
        if d:
            head_copy(d).wait_recv()
        shard = og_ref[...] if d == 0 else ogbuf[d - 1]
        weight = wbuf[:, pl.ds(pl.multiple_of(source * cols, cols), cols)]
        product = lax.dot_general(
            shard, weight, (((1,), (1,)), ((), ())), preferred_element_type=jnp.float32
        )
        if d == 0:
            acc[...] = product
        else:
            acc[...] += product

    run(lambda c: c.start(), False)
    do_ref[...] = acc[...].astype(jnp.bfloat16)
    run(lambda c: c.wait_send(), True)
    for d in range(1, HN):
        head_copy(d).wait_send()


def local_kernel(rb, gb, q_ref, kv_ref, do_ref, w_ref, out_ref, dq_ref, dkv_ref, acc, att_ref):
    me = lax.axis_index("ctx")
    group = lax.axis_index("head")
    nblk = kv_ref.shape[0]
    blocks = q_ref.shape[0] // BLK
    width = q_ref.shape[1]
    heads = width // HD
    scaling = HD ** (-0.5)
    acc[...] = jnp.zeros_like(acc)
    nt = (((1,), (1,)), ((), ()))
    tn = (((0,), (0,)), ((), ()))
    nn = (((1,), (0,)), ((), ()))

    def dot(a, b, dims):
        return lax.dot_general(a, b, dims, preferred_element_type=jnp.float32)

    def step(n, carry):
        i = me * blocks + n
        rows = pl.ds(pl.multiple_of(n * BLK, BLK), BLK)
        column = lax.broadcasted_iota(jnp.int32, (BLK, 8 * BLK), 1)
        first_end = jnp.where(i == 0, BLK, 0)
        last_end = jnp.where(i == nblk - 1, 3 * BLK, 2 * BLK)
        dead = (column < first_end) | ((column >= 2 * BLK) & (column < last_end))
        for h in range(heads):
            hc = slice(h * HD, (h + 1) * HD)
            vc = slice(width + h * HD, width + (h + 1) * HD)
            base = ((group * heads + h) * nblk + i) * R
            ids = [jnp.maximum(i - 1, 0), i, jnp.minimum(i + 1, nblk - 1), gb[0], gb[1]]
            ids = ids + [rb[base + r] for r in range(R)]
            kg = jnp.concatenate([kv_ref[e, :, hc] for e in ids], axis=0)
            vg = jnp.concatenate([kv_ref[e, :, vc] for e in ids], axis=0)
            q = q_ref[rows, hc]
            do = do_ref[rows, hc]
            logits = jnp.where(dead, -jnp.inf, dot(q, kg, nt) * scaling)
            e = jnp.exp(logits - jnp.max(logits, axis=1, keepdims=True))
            weights = e * (1.0 / jnp.sum(e, axis=1, keepdims=True))
            low = weights.astype(jnp.bfloat16)
            att = dot(low, vg, nn).astype(jnp.bfloat16)
            att_ref[rows, hc] = att
            delta = jnp.sum(do.astype(jnp.float32) * att.astype(jnp.float32), axis=1, keepdims=True)
            lg = (weights * (dot(do, vg, nt) - delta)).astype(jnp.bfloat16)
            dq_ref[rows, hc] = (dot(lg, kg, nn) * scaling).astype(jnp.bfloat16)
            dk = dot(lg, q, tn) * scaling
            dv = dot(low, do, tn)
            for k, e in enumerate(ids):
                acc[e, :, hc] += dk[k * BLK : (k + 1) * BLK]
                acc[e, :, vc] += dv[k * BLK : (k + 1) * BLK]
        return carry

    lax.fori_loop(0, blocks, step, 0)
    cols = out_ref.shape[2]
    for j in range(out_ref.shape[0]):
        out_ref[j] = dot(att_ref[...], w_ref[:, j * cols : (j + 1) * cols], nn).astype(jnp.bfloat16)
    dkv_ref[...] = acc[...].astype(jnp.bfloat16)


def reduce_kernel(part_ref, outp_ref, out_ref, dk_ref, dv_ref, acc, rz, ry, ro, sums, ssem, zsem, ysem, hs, hr):
    me = lax.axis_index("ctx")
    head = lax.axis_index("head")
    z, y = me // YN, lax.rem(me, YN)
    width = dk_ref.shape[1]
    greet(z, y, head)

    def head_copy(d):
        target = lax.rem(head + d, HN)
        return pltpu.make_async_remote_copy(
            src_ref=outp_ref.at[target],
            dst_ref=ro.at[d - 1],
            send_sem=hs.at[d - 1],
            recv_sem=hr.at[d - 1],
            device_id={"head": target},
            device_id_type=MESH,
        )

    def span(p):
        return pl.ds(PARTS[p][0], PARTS[p][1] - PARTS[p][0])

    def zcopy(way, slot, p):
        return pltpu.make_async_remote_copy(
            src_ref=acc.at[slot, span(p)],
            dst_ref=rz.at[way, slot, span(p)],
            send_sem=ssem.at[slot * NP + p],
            recv_sem=zsem.at[(way * 8 + slot) * NP + p],
            device_id={"ctx": (jnp.minimum(z + 1, ZN - 1) if way == 0 else jnp.maximum(z - 1, 0)) * YN + y},
            device_id_type=MESH,
        )

    def ycopy(source, zd, p):
        return pltpu.make_async_remote_copy(
            src_ref=source.at[zd * YN + (1 - y), span(p)],
            dst_ref=ry.at[zd, span(p)],
            send_sem=ssem.at[(zd * YN + (1 - y)) * NP + p],
            recv_sem=ysem.at[zd * NP + p],
            device_id={"ctx": z * YN + (1 - y)},
            device_id_type=MESH,
        )

    def zadd(way, slot, p, total):
        zcopy(way, slot, p).wait_recv()
        return total + rz[way, slot, span(p)].astype(jnp.float32)

    def far(act):
        for t in range(ZN - 1, -1, -1):
            for way in range(2):
                if t == 0 and way:
                    continue
                zd = z + t if way == 0 else z - t

                @pl.when((zd >= 0) & (zd < ZN))
                def _():
                    act(zd, way, t)

    bulk = [p for p in range(NP) if not PARTS[p][2]]
    fast = [p for p in range(NP) if PARTS[p][2]]

    def start_y(zd, way, t):
        for p in bulk:
            ycopy(part_ref, zd, p).start()

    far(start_y)
    for d in range(1, HN):
        head_copy(d).start()

    def pass_z(zd, way, t):
        if t == 0:
            return
        behind = z > 0 if way == 0 else z < ZN - 1
        for slot, p in [(zd * YN + (1 - y), p) for p in fast] + [(zd * YN + y, p) for p in range(NP)]:
            total = part_ref[slot, span(p)].astype(jnp.float32)
            if not PARTS[p][2]:
                ycopy(part_ref, zd, p).wait_recv()
                total = total + ry[zd, span(p)].astype(jnp.float32)
            acc[slot, span(p)] = total.astype(jnp.bfloat16)

            @pl.when(behind)
            def _():
                acc[slot, span(p)] = zadd(way, slot, p, acc[slot, span(p)].astype(jnp.float32)).astype(
                    jnp.bfloat16
                )

            zcopy(way, slot, p).start()

    far(pass_z)

    def settle(slot, p):
        sums[span(p)] = part_ref[slot, span(p)].astype(jnp.float32)

        @pl.when(z > 0)
        def _():
            sums[span(p)] = zadd(0, slot, p, sums[span(p)])

        @pl.when(z < ZN - 1)
        def _():
            sums[span(p)] = zadd(1, slot, p, sums[span(p)])

    other = z * YN + (1 - y)
    for p in fast:
        settle(other, p)
        acc[other, span(p)] = sums[span(p)].astype(jnp.bfloat16)
        ycopy(acc, z, p).start()
    total = outp_ref[head].astype(jnp.float32)
    for d in range(1, HN):
        head_copy(d).wait_recv()
        total = total + ro[d - 1].astype(jnp.float32)
    out_ref[...] = total.astype(jnp.bfloat16)
    for p in bulk + fast:
        settle(me, p)
        ycopy(part_ref if p in bulk else acc, z, p).wait_recv()
        grad = sums[span(p)] + ry[z, span(p)].astype(jnp.float32)
        dk_ref[span(p)] = grad[:, :width].astype(jnp.bfloat16)
        dv_ref[span(p)] = grad[:, width:].astype(jnp.bfloat16)

    def end_y(zd, way, t):
        for p in bulk:
            ycopy(part_ref, zd, p).wait_send()

    def end_z(zd, way, t):
        if t == 0:
            return
        for slot, p in [(zd * YN + (1 - y), p) for p in fast] + [(zd * YN + y, p) for p in range(NP)]:
            zcopy(way, slot, p).wait_send()

    far(end_y)
    far(end_z)
    for p in fast:
        ycopy(acc, z, p).wait_send()
    for d in range(1, HN):
        head_copy(d).wait_send()


def near_body(queries, keys, values, output_grad, out_weight, random_blocks, global_blocks):
    rows, width = queries.shape
    cols = output_grad.shape[1]
    cn = YN * ZN
    vmem = pl.BlockSpec(memory_space=pltpu.VMEM)
    smem = pl.BlockSpec(memory_space=pltpu.SMEM)
    anywhere = pl.BlockSpec(memory_space=pl.ANY)
    bf16, f32 = jnp.bfloat16, jnp.float32
    dma = pltpu.SemaphoreType.DMA
    kv, grad = pl.pallas_call(
        gather_kernel,
        name="gather",
        out_shape=(
            jax.ShapeDtypeStruct((cn, rows, 2 * width), bf16),
            jax.ShapeDtypeStruct((rows, width), bf16),
        ),
        in_specs=[vmem, vmem, vmem, anywhere],
        out_specs=(vmem, vmem),
        scratch_shapes=[
            pltpu.VMEM((HN - 1, rows, cols), bf16),
            pltpu.VMEM(out_weight.shape, bf16),
            pltpu.VMEM((rows, width), f32),
            dma,
            dma((3 * cn * NP,)),
            dma((cn * NP,)),
            dma((HN - 1,)),
            dma((HN - 1,)),
        ],
        compiler_params=pltpu.CompilerParams(
            collective_id=0, has_side_effects=True, vmem_limit_bytes=32 << 20
        ),
    )(keys, values, output_grad, out_weight)
    nblk = cn * rows // BLK
    outp, dq, part = pl.pallas_call(
        local_kernel,
        name="attention",
        out_shape=(
            jax.ShapeDtypeStruct((HN, rows, cols), bf16),
            jax.ShapeDtypeStruct((rows, width), bf16),
            jax.ShapeDtypeStruct((nblk, BLK, 2 * width), bf16),
        ),
        in_specs=[smem, smem, vmem, vmem, vmem, vmem],
        out_specs=(vmem, vmem, vmem),
        scratch_shapes=[pltpu.VMEM((nblk, BLK, 2 * width), f32), pltpu.VMEM((rows, width), bf16)],
        compiler_params=pltpu.CompilerParams(vmem_limit_bytes=48 << 20),
    )(
        random_blocks.reshape(-1),
        global_blocks,
        queries,
        kv.reshape(nblk, BLK, 2 * width),
        grad,
        out_weight,
    )
    out, dk, dv = pl.pallas_call(
        reduce_kernel,
        name="reduce",
        out_shape=(
            jax.ShapeDtypeStruct((rows, cols), bf16),
            jax.ShapeDtypeStruct((rows, width), bf16),
            jax.ShapeDtypeStruct((rows, width), bf16),
        ),
        in_specs=[vmem, vmem],
        out_specs=(vmem, vmem, vmem),
        scratch_shapes=[
            pltpu.VMEM((cn, rows, 2 * width), bf16),
            pltpu.VMEM((2, cn, rows, 2 * width), bf16),
            pltpu.VMEM((ZN, rows, 2 * width), bf16),
            pltpu.VMEM((HN - 1, rows, cols), bf16),
            pltpu.VMEM((rows, 2 * width), f32),
            dma((cn * NP,)),
            dma((2 * cn * NP,)),
            dma((ZN * NP,)),
            dma((HN - 1,)),
            dma((HN - 1,)),
        ],
        compiler_params=pltpu.CompilerParams(
            collective_id=1, has_side_effects=True, vmem_limit_bytes=48 << 20
        ),
    )(part.reshape(cn, rows, 2 * width), outp)
    return (out, dq, dk, dv)


def solution(mesh):
    near = mesh.shape["ctx"] == YN * ZN and mesh.shape["head"] == HN
    placed = (
        P("ctx", "head"),
        P("ctx", "head"),
        P("ctx", "head"),
        P("ctx", "head"),
        P("head", None),
        P(),
        P(),
    )
    return jax.shard_map(
        near_body if near else body,
        mesh=mesh,
        in_specs=placed,
        out_specs=(P("ctx", "head"), P("ctx", "head"), P("ctx", "head"), P("ctx", "head")),
        check_vma=False,
    )
```

```python
import functools

import jax
import jax.numpy as jnp
from jax import lax
from jax.experimental import pallas as pl
from jax.experimental.pallas import tpu as pltpu
from jax.sharding import PartitionSpec as P

HD = 128
BLK = 64
R = 3
G = 2


def with_halo(cells, sides, width):
    for axis, dim in sides:
        count = lax.axis_size(axis)
        ends = count - 1
        head = lax.slice_in_dim(cells, 0, width, axis=dim)
        tail = lax.slice_in_dim(cells, cells.shape[dim] - width, cells.shape[dim], axis=dim)
        cells = jnp.concatenate(
            [
                lax.ppermute(tail, axis, [(i, (i + 1) % count) for i in range(ends)]),
                cells,
                lax.ppermute(head, axis, [((i + 1) % count, i) for i in range(ends)]),
            ],
            axis=dim,
        )
    return cells


def send_plan(request_table, shards, blocks, my_shard):
    requests = request_table.shape[1]
    owners = request_table // blocks
    within = request_table % blocks
    request_ids = jnp.arange(requests, dtype=jnp.int32)
    earlier = (owners[:, :, None] == owners[:, None, :]) & (
        request_ids[None, None, :] < request_ids[None, :, None]
    )
    ranking = jnp.sum(earlier.astype(jnp.int32), axis=2)
    capacity = (requests + shards - 2) // (shards - 1)
    slot_ids = jnp.arange(capacity, dtype=jnp.int32)
    owned = (owners == my_shard)[:, None, :] & (ranking[:, None, :] == slot_ids[None, :, None])
    tile_ids = (request_ids // (blocks * R))[None, :] * blocks + within
    send_tiles = jnp.sum(jnp.where(owned, tile_ids[:, None, :], 0), axis=2).reshape(-1)
    send_alive = jnp.any(owned, axis=2).reshape(-1)
    my_owners = lax.dynamic_index_in_dim(owners, my_shard, 0, keepdims=False)
    my_ranks = lax.dynamic_index_in_dim(ranking, my_shard, 0, keepdims=False)
    return (send_tiles, send_alive, my_owners * capacity + my_ranks)


def pick_tiles(pair_tiles, send_tiles, blocks):
    return pair_tiles[send_tiles % blocks, :, send_tiles // blocks, :]


def pair_products(row_tiles, window, global_pairs, fetched, low_edge, high_edge):
    nearby = jnp.einsum(
        "nqhd,nwbhd->nhqwb",
        row_tiles,
        window[..., low_edge:high_edge],
        preferred_element_type=jnp.float32,
    )
    distant = jnp.einsum(
        "nqhd,gbhd->nhqgb",
        row_tiles,
        global_pairs[..., low_edge:high_edge],
        preferred_element_type=jnp.float32,
    )
    chance = jnp.einsum(
        "nqhd,hnrbd->nhqrb",
        row_tiles,
        fetched[..., low_edge:high_edge],
        preferred_element_type=jnp.float32,
    )
    return jnp.concatenate([nearby, distant, chance], axis=3)


def collect_rows(mixing, window, global_pairs, fetched, low_edge, high_edge):
    nearby = jnp.einsum(
        "nhqwb,nwbhd->nqhd",
        mixing[:, :, :, :3],
        window[..., low_edge:high_edge],
        preferred_element_type=jnp.float32,
    )
    distant = jnp.einsum(
        "nhqgb,gbhd->nqhd",
        mixing[:, :, :, 3 : 3 + G],
        global_pairs[..., low_edge:high_edge],
        preferred_element_type=jnp.float32,
    )
    chance = jnp.einsum(
        "nhqrb,hnrbd->nqhd",
        mixing[:, :, :, 3 + G :],
        fetched[..., low_edge:high_edge],
        preferred_element_type=jnp.float32,
    )
    return nearby + distant + chance


def tile_terms(mixing, row_tiles):
    nearby = jnp.einsum(
        "nhqwb,nqhd->nwbhd", mixing[:, :, :, :3], row_tiles, preferred_element_type=jnp.float32
    )
    distant = jnp.einsum(
        "nhqgb,nqhd->gbhd",
        mixing[:, :, :, 3 : 3 + G],
        row_tiles,
        preferred_element_type=jnp.float32,
    )
    chance = jnp.einsum(
        "nhqrb,nqhd->hnrbd", mixing[:, :, :, 3 + G :], row_tiles, preferred_element_type=jnp.float32
    )
    return (nearby, distant, chance)


def body(queries, keys, values, output_grad, out_weight, random_blocks, global_blocks):
    shards = lax.axis_size("ctx")
    my_shard = lax.axis_index("ctx")
    head_group = lax.axis_index("head")
    tok_local, width_local = queries.shape
    head_dim = HD
    heads_local = width_local // head_dim
    blocks = tok_local // BLK
    scaling = head_dim ** (-0.5)
    query_tiles = queries.reshape(blocks, BLK, heads_local, head_dim)
    pair_tiles = jnp.concatenate(
        [
            keys.reshape(blocks, BLK, heads_local, head_dim),
            values.reshape(blocks, BLK, heads_local, head_dim),
        ],
        axis=3,
    )
    head_table = lax.dynamic_slice_in_dim(random_blocks, head_group * heads_local, heads_local, 0)
    request_table = (
        head_table.reshape(heads_local, shards, blocks, R)
        .transpose(1, 0, 2, 3)
        .reshape(shards, heads_local * blocks * R)
    )
    send_tiles, send_alive, receive_rows = send_plan(request_table, shards, blocks, my_shard)
    received = lax.all_to_all(
        pick_tiles(pair_tiles, send_tiles, blocks), "ctx", split_axis=0, concat_axis=0, tiled=True
    )
    fetched = received[receive_rows].reshape(heads_local, blocks, R, BLK, 2 * head_dim)
    padded = with_halo(pair_tiles.reshape(tok_local, 2 * width_local), (("ctx", 0),), BLK)
    padded = padded.reshape(blocks + 2, BLK, heads_local, 2 * head_dim)
    window = jnp.stack([padded[offset : offset + blocks] for offset in range(3)], axis=1)
    global_owner = global_blocks // blocks
    global_local = global_blocks % blocks
    picked = pair_tiles[global_local]
    holding = jnp.where(
        (global_owner == my_shard)[:, None, None, None], picked.astype(jnp.float32), 0.0
    )
    global_pairs = lax.psum(holding, "ctx").astype(jnp.bfloat16)
    first_block = my_shard * blocks
    window_ids = first_block + jnp.arange(blocks)[:, None] + jnp.arange(3)[None, :] - 1
    inside = (window_ids >= 0) & (window_ids < blocks * shards)
    alive_mask = jnp.concatenate([inside, jnp.ones((blocks, G + R), dtype=bool)], axis=1)[
        :, None, None, :, None
    ]
    logits = jnp.where(
        alive_mask,
        pair_products(query_tiles, window, global_pairs, fetched, 0, head_dim) * scaling,
        -jnp.inf,
    )
    row_max = jnp.max(logits, axis=(3, 4))
    log_total = row_max + jnp.log(jnp.sum(jnp.exp(logits - row_max[..., None, None]), axis=(3, 4)))
    weights_full = jnp.exp(logits - log_total[..., None, None])
    weights_low = weights_full.astype(jnp.bfloat16)
    attended = collect_rows(
        weights_low, window, global_pairs, fetched, head_dim, 2 * head_dim
    ).astype(jnp.bfloat16)
    attended_flat = attended.reshape(tok_local, width_local)
    partial_value = jnp.dot(attended_flat, out_weight, preferred_element_type=jnp.float32)
    output = lax.psum_scatter(partial_value, "head", scatter_dimension=1, tiled=True).astype(
        jnp.bfloat16
    )
    grad_sum = lax.dot_general(
        lax.all_gather(output_grad, "head", axis=1, tiled=True),
        out_weight,
        (((1,), (1,)), ((), ())),
        preferred_element_type=jnp.float32,
    )
    grad_tiles = grad_sum.astype(jnp.bfloat16).reshape(blocks, BLK, heads_local, head_dim)
    delta_rows = jnp.sum(
        grad_tiles.astype(jnp.float32) * attended.astype(jnp.float32), axis=3
    ).transpose(0, 2, 1)
    products = pair_products(grad_tiles, window, global_pairs, fetched, head_dim, 2 * head_dim)
    logit_grad = (weights_full * (products - delta_rows[..., None, None])).astype(jnp.bfloat16)
    query_grad = (
        (collect_rows(logit_grad, window, global_pairs, fetched, 0, head_dim) * scaling)
        .astype(jnp.bfloat16)
        .reshape(tok_local, width_local)
    )
    key_nearby, key_distant, key_chance = tile_terms(logit_grad, query_tiles)
    value_nearby, value_distant, value_chance = tile_terms(weights_low, grad_tiles)
    nearby_terms = jnp.concatenate([key_nearby * scaling, value_nearby], axis=4)
    framed = sum(
        (
            jnp.pad(nearby_terms[:, offset], ((offset, 2 - offset), (0, 0), (0, 0), (0, 0)))
            for offset in range(3)
        )
    )
    edge_rows = jnp.concatenate([framed[0], framed[blocks + 1]], axis=0).reshape(
        2 * BLK, 2 * width_local
    )
    arrived = with_halo(edge_rows.astype(jnp.bfloat16), (("ctx", 0),), BLK).astype(edge_rows.dtype)
    local_grad = framed[1 : blocks + 1]
    local_grad = local_grad.at[0].add(arrived[:BLK].reshape(BLK, heads_local, 2 * head_dim))
    local_grad = local_grad.at[blocks - 1].add(
        arrived[3 * BLK :].reshape(BLK, heads_local, 2 * head_dim)
    )
    distant_terms = jnp.concatenate([key_distant * scaling, value_distant], axis=3)
    summed = lax.psum(distant_terms, "ctx")
    selector = (
        (global_owner == my_shard)[:, None] & (global_local[:, None] == jnp.arange(blocks)[None, :])
    ).astype(jnp.float32)
    local_grad = local_grad + jnp.einsum(
        "gn,gbhd->nbhd", selector, summed, precision=lax.Precision.HIGHEST
    )
    chance_terms = (
        jnp.concatenate([key_chance * scaling, value_chance], axis=4)
        .astype(jnp.bfloat16)
        .reshape(-1, BLK, 2 * head_dim)
    )
    outgoing_grads = (
        jnp.zeros((send_tiles.shape[0], BLK, 2 * head_dim), jnp.bfloat16)
        .at[receive_rows]
        .set(chance_terms)
    )
    returned = lax.all_to_all(outgoing_grads, "ctx", split_axis=0, concat_axis=0, tiled=True)
    segment_ids = jnp.where(send_alive, send_tiles, heads_local * blocks)
    gathered = jax.ops.segment_sum(
        returned.astype(jnp.float32), segment_ids, num_segments=heads_local * blocks + 1
    )[: heads_local * blocks]
    local_grad = local_grad + gathered.reshape(heads_local, blocks, BLK, 2 * head_dim).transpose(
        1, 2, 0, 3
    )
    key_grad = local_grad[..., :head_dim].astype(jnp.bfloat16).reshape(tok_local, width_local)
    value_grad = local_grad[..., head_dim:].astype(jnp.bfloat16).reshape(tok_local, width_local)
    return (output, query_grad, key_grad, value_grad)


MESH = pl.DeviceIdType.MESH
YN = 2
ZN = 4
HN = 4
PARTS = ((0, 48, True), (48, 128, False), (128, 192, False), (192, 256, False))
NP = len(PARTS)


def greet(z, y, head):
    bar = pltpu.get_barrier_semaphore()

    def hello(target):
        pl.semaphore_signal(bar, inc=1, device_id=target, device_id_type=MESH)

    hello({"ctx": z * YN + (1 - y)})
    for d in range(1, HN):
        hello({"head": lax.rem(head + d, HN)})

    @pl.when(z > 0)
    def _():
        hello({"ctx": (z - 1) * YN + y})

    @pl.when(z < ZN - 1)
    def _():
        hello({"ctx": (z + 1) * YN + y})

    lower = jnp.where(z > 0, 1, 0)
    upper = jnp.where(z < ZN - 1, 1, 0)
    pl.semaphore_wait(bar, HN + lower + upper)


def gather_kernel(k_ref, v_ref, og_ref, w_hbm, kv_ref, do_ref, wbuf, ogbuf, oglocal, acc, wsem, lsem, ssem, rsem, hs, hr):
    me = lax.axis_index("ctx")
    head = lax.axis_index("head")
    z, y = me // YN, lax.rem(me, YN)
    width = k_ref.shape[1]
    cols = og_ref.shape[1]
    wcopy = pltpu.make_async_copy(w_hbm, wbuf, wsem)
    wcopy.start()
    kcopy = pltpu.make_async_copy(k_ref, kv_ref.at[me, :, pl.ds(0, width)], lsem.at[0])
    vcopy = pltpu.make_async_copy(v_ref, kv_ref.at[me, :, pl.ds(width, width)], lsem.at[1])
    ogcopy = pltpu.make_async_copy(og_ref, oglocal, lsem.at[2])
    kcopy.start()
    vcopy.start()
    ogcopy.start()
    greet(z, y, head)
    kcopy.wait()
    vcopy.wait()

    def copy(way, slot, p):
        lo, hi, _ = PARTS[p]
        at = kv_ref.at[slot, pl.ds(lo, hi - lo)]
        target = (z + 1) * YN + y if way == 0 else (z - 1) * YN + y if way == 1 else z * YN + (1 - y)
        return pltpu.make_async_remote_copy(
            src_ref=at,
            dst_ref=at,
            send_sem=ssem.at[(way * 8 + slot) * NP + p],
            recv_sem=rsem.at[slot * NP + p],
            device_id={"ctx": target},
            device_id_type=MESH,
        )

    def onward(way, slot, p, act):
        inside = z < ZN - 1 if way == 0 else z > 0

        @pl.when(inside)
        def _():
            act(copy(way, slot, p))

    def run(act, waiting):
        for p in range(NP):
            act(copy(2, me, p))
            onward(0, me, p, act)
            onward(1, me, p, act)
        if not waiting:
            send_heads()
            multiply(0)
        other = z * YN + (1 - y)
        for p in range(NP):
            if PARTS[p][2]:
                if not waiting:
                    copy(2, other, p).wait_recv()
                onward(0, other, p, act)
                onward(1, other, p, act)
        for t in range(1, ZN):
            for p in range(NP):
                for way in range(2):
                    zs = z - t if way == 0 else z + t

                    @pl.when((zs >= 0) & (zs < ZN))
                    def _():
                        slot = zs * YN + y
                        if not waiting:
                            copy(2, slot, p).wait_recv()
                        onward(way, slot, p, act)
                        if PARTS[p][2]:
                            over = zs * YN + (1 - y)
                            if not waiting:
                                copy(2, over, p).wait_recv()
                            onward(way, over, p, act)
                        else:
                            act(copy(2, slot, p))
            if not waiting:
                multiply(t)
        if not waiting:
            for zs in range(ZN):
                for p in range(NP):
                    if not PARTS[p][2]:
                        copy(2, zs * YN + (1 - y), p).wait_recv()

    order = (0, 1, 2, 3)

    def head_copy(d):
        return pltpu.make_async_remote_copy(
            src_ref=og_ref,
            dst_ref=ogbuf.at[d - 1],
            send_sem=hs.at[d - 1],
            recv_sem=hr.at[d - 1],
            device_id={"head": lax.rem(head + d, HN)},
            device_id_type=MESH,
        )

    def send_heads():
        for d in range(1, HN):
            head_copy(d).start()
        ogcopy.wait()
        wcopy.wait()

    def multiply(d):
        source = lax.rem(head - order[d] + HN, HN)
        if d:
            head_copy(d).wait_recv()
        shard = oglocal[...] if d == 0 else ogbuf[d - 1]
        weight = wbuf[:, pl.ds(pl.multiple_of(source * cols, cols), cols)]
        product = lax.dot_general(
            shard, weight, (((1,), (1,)), ((), ())), preferred_element_type=jnp.float32
        )
        if d == 0:
            acc[...] = product
        else:
            acc[...] += product

    run(lambda c: c.start(), False)
    do_ref[...] = acc[...].astype(jnp.bfloat16)
    run(lambda c: c.wait_send(), True)
    for d in range(1, HN):
        head_copy(d).wait_send()


def local_kernel(rb, gb, q_ref, kv_ref, do_ref, w_ref, out_ref, dq_ref, dkv_ref, shared, att_ref):
    me = lax.axis_index("ctx")
    group = lax.axis_index("head")
    nblk = kv_ref.shape[0]
    blocks = q_ref.shape[0] // BLK
    width = q_ref.shape[1]
    heads = width // HD
    scaling = HD ** (-0.5)
    dkv_ref[...] = jnp.zeros_like(dkv_ref)
    shared[...] = jnp.zeros_like(shared)
    nt = (((1,), (1,)), ((), ()))
    tn = (((0,), (0,)), ((), ()))
    nn = (((1,), (0,)), ((), ()))

    def dot(a, b, dims):
        return lax.dot_general(a, b, dims, preferred_element_type=jnp.float32)

    def step(n, carry):
        i = me * blocks + n
        rows = pl.ds(pl.multiple_of(n * BLK, BLK), BLK)
        column = lax.broadcasted_iota(jnp.int32, (BLK, 8 * BLK), 1)
        first_end = jnp.where(i == 0, BLK, 0)
        last_end = jnp.where(i == nblk - 1, 3 * BLK, 2 * BLK)
        dead = (column < first_end) | ((column >= 2 * BLK) & (column < last_end))
        late = []
        for h in range(heads):
            hc = slice(h * HD, (h + 1) * HD)
            vc = slice(width + h * HD, width + (h + 1) * HD)
            ids = [jnp.maximum(i - 1, 0), i, jnp.minimum(i + 1, nblk - 1), gb[0], gb[1]]
            ids = ids + [rb[r, group * heads + h, i] for r in range(R)]
            kg = jnp.concatenate([kv_ref[e, :, hc] for e in ids], axis=0)
            vg = jnp.concatenate([kv_ref[e, :, vc] for e in ids], axis=0)
            q = q_ref[rows, hc]
            do = do_ref[rows, hc]
            logits = jnp.where(dead, -jnp.inf, dot(q, kg, nt) * scaling)
            e = jnp.exp(logits - jnp.max(logits, axis=1, keepdims=True))
            weights = e * (1.0 / jnp.sum(e, axis=1, keepdims=True))
            low = weights.astype(jnp.bfloat16)
            att = dot(low, vg, nn).astype(jnp.bfloat16)
            att_ref[rows, hc] = att
            delta = jnp.sum(do.astype(jnp.float32) * att.astype(jnp.float32), axis=1, keepdims=True)
            lg = (weights * (dot(do, vg, nt) - delta)).astype(jnp.bfloat16)
            dq_ref[rows, hc] = (dot(lg, kg, nn) * scaling).astype(jnp.bfloat16)
            dk = dot(lg, q, tn) * scaling
            dv = dot(low, do, tn)
            late.append((hc, vc, ids, dk, dv))
        for hc, vc, ids, dk, dv in late:
            for g in range(G):
                shared[g, :, hc] += dk[(3 + g) * BLK : (4 + g) * BLK]
                shared[g, :, vc] += dv[(3 + g) * BLK : (4 + g) * BLK]
            for k in (0, 1, 2, 5, 6, 7):
                for at, term in ((hc, dk), (vc, dv)):
                    held = dkv_ref[ids[k], :, at].astype(jnp.float32)
                    held = held + term[k * BLK : (k + 1) * BLK]
                    dkv_ref[ids[k], :, at] = held.astype(jnp.bfloat16)
        return carry

    lax.fori_loop(0, blocks, step, 0)
    cols = out_ref.shape[2]
    for j in range(out_ref.shape[0]):
        out_ref[j] = dot(att_ref[...], w_ref[:, j * cols : (j + 1) * cols], nn).astype(jnp.bfloat16)
    for g in range(G):
        held = dkv_ref[gb[g]].astype(jnp.float32)
        dkv_ref[gb[g]] = (held + shared[g]).astype(jnp.bfloat16)


def reduce_kernel(part_ref, outp_ref, out_ref, dk_ref, dv_ref, acc, rz, ry, ro, sums, ssem, zsem, ysem, hs, hr):
    me = lax.axis_index("ctx")
    head = lax.axis_index("head")
    z, y = me // YN, lax.rem(me, YN)
    width = dk_ref.shape[1]
    greet(z, y, head)

    def head_copy(d):
        target = lax.rem(head + d, HN)
        return pltpu.make_async_remote_copy(
            src_ref=outp_ref.at[target],
            dst_ref=ro.at[d - 1],
            send_sem=hs.at[d - 1],
            recv_sem=hr.at[d - 1],
            device_id={"head": target},
            device_id_type=MESH,
        )

    def span(p):
        return pl.ds(PARTS[p][0], PARTS[p][1] - PARTS[p][0])

    def zcopy(way, slot, p):
        return pltpu.make_async_remote_copy(
            src_ref=acc.at[slot, span(p)],
            dst_ref=rz.at[way, slot, span(p)],
            send_sem=ssem.at[slot * NP + p],
            recv_sem=zsem.at[(way * 8 + slot) * NP + p],
            device_id={"ctx": (jnp.minimum(z + 1, ZN - 1) if way == 0 else jnp.maximum(z - 1, 0)) * YN + y},
            device_id_type=MESH,
        )

    def ycopy(source, zd, p):
        return pltpu.make_async_remote_copy(
            src_ref=source.at[zd * YN + (1 - y), span(p)],
            dst_ref=ry.at[zd, span(p)],
            send_sem=ssem.at[(zd * YN + (1 - y)) * NP + p],
            recv_sem=ysem.at[zd * NP + p],
            device_id={"ctx": z * YN + (1 - y)},
            device_id_type=MESH,
        )

    def zadd(way, slot, p, total):
        zcopy(way, slot, p).wait_recv()
        return total + rz[way, slot, span(p)].astype(jnp.float32)

    def far(act):
        for t in range(ZN - 1, -1, -1):
            for way in range(2):
                if t == 0 and way:
                    continue
                zd = z + t if way == 0 else z - t

                @pl.when((zd >= 0) & (zd < ZN))
                def _():
                    act(zd, way, t)

    bulk = [p for p in range(NP) if not PARTS[p][2]]
    fast = [p for p in range(NP) if PARTS[p][2]]

    def start_y(zd, way, t):
        for p in bulk:
            ycopy(part_ref, zd, p).start()

    far(start_y)
    for d in range(1, HN):
        head_copy(d).start()

    def pass_z(zd, way, t):
        if t == 0:
            return
        behind = z > 0 if way == 0 else z < ZN - 1
        for slot, p in [(zd * YN + (1 - y), p) for p in fast] + [(zd * YN + y, p) for p in range(NP)]:
            total = part_ref[slot, span(p)].astype(jnp.float32)
            if not PARTS[p][2]:
                ycopy(part_ref, zd, p).wait_recv()
                total = total + ry[zd, span(p)].astype(jnp.float32)
            acc[slot, span(p)] = total.astype(jnp.bfloat16)

            @pl.when(behind)
            def _():
                acc[slot, span(p)] = zadd(way, slot, p, acc[slot, span(p)].astype(jnp.float32)).astype(
                    jnp.bfloat16
                )

            zcopy(way, slot, p).start()

    far(pass_z)

    def settle(slot, p):
        sums[span(p)] = part_ref[slot, span(p)].astype(jnp.float32)

        @pl.when(z > 0)
        def _():
            sums[span(p)] = zadd(0, slot, p, sums[span(p)])

        @pl.when(z < ZN - 1)
        def _():
            sums[span(p)] = zadd(1, slot, p, sums[span(p)])

    other = z * YN + (1 - y)
    for p in fast:
        settle(other, p)
        acc[other, span(p)] = sums[span(p)].astype(jnp.bfloat16)
        ycopy(acc, z, p).start()
    total = outp_ref[head].astype(jnp.float32)
    for d in range(1, HN):
        head_copy(d).wait_recv()
        total = total + ro[d - 1].astype(jnp.float32)
    out_ref[...] = total.astype(jnp.bfloat16)
    for p in bulk + fast:
        settle(me, p)
        ycopy(part_ref if p in bulk else acc, z, p).wait_recv()
        grad = sums[span(p)] + ry[z, span(p)].astype(jnp.float32)
        dk_ref[span(p)] = grad[:, :width].astype(jnp.bfloat16)
        dv_ref[span(p)] = grad[:, width:].astype(jnp.bfloat16)

    def end_y(zd, way, t):
        for p in bulk:
            ycopy(part_ref, zd, p).wait_send()

    def end_z(zd, way, t):
        if t == 0:
            return
        for slot, p in [(zd * YN + (1 - y), p) for p in fast] + [(zd * YN + y, p) for p in range(NP)]:
            zcopy(way, slot, p).wait_send()

    far(end_y)
    far(end_z)
    for p in fast:
        ycopy(acc, z, p).wait_send()
    for d in range(1, HN):
        head_copy(d).wait_send()


def near_body(queries, keys, values, output_grad, out_weight, random_blocks, global_blocks):
    rows, width = queries.shape
    cols = output_grad.shape[1]
    cn = YN * ZN
    vmem = pl.BlockSpec(memory_space=pltpu.VMEM)
    smem = pl.BlockSpec(memory_space=pltpu.SMEM)
    hbm = pl.BlockSpec(memory_space=pltpu.HBM)
    bf16, f32 = jnp.bfloat16, jnp.float32
    dma = pltpu.SemaphoreType.DMA
    kv, grad, weight = pl.pallas_call(
        gather_kernel,
        name="gather",
        out_shape=(
            jax.ShapeDtypeStruct((cn, rows, 2 * width), bf16),
            jax.ShapeDtypeStruct((rows, width), bf16),
            jax.ShapeDtypeStruct(out_weight.shape, bf16),
        ),
        in_specs=[hbm, hbm, hbm, hbm],
        out_specs=(vmem, vmem, vmem),
        scratch_shapes=[
            pltpu.VMEM((HN - 1, rows, cols), bf16),
            pltpu.VMEM((rows, cols), bf16),
            pltpu.VMEM((rows, width), f32),
            dma,
            dma((3,)),
            dma((3 * cn * NP,)),
            dma((cn * NP,)),
            dma((HN - 1,)),
            dma((HN - 1,)),
        ],
        compiler_params=pltpu.CompilerParams(
            collective_id=0, has_side_effects=True, vmem_limit_bytes=16 << 20
        ),
    )(keys, values, output_grad, out_weight)
    nblk = cn * rows // BLK
    outp, dq, part = pl.pallas_call(
        local_kernel,
        name="attention",
        out_shape=(
            jax.ShapeDtypeStruct((HN, rows, cols), bf16),
            jax.ShapeDtypeStruct((rows, width), bf16),
            jax.ShapeDtypeStruct((nblk, BLK, 2 * width), bf16),
        ),
        in_specs=[smem, smem, vmem, vmem, vmem, vmem],
        out_specs=(vmem, vmem, vmem),
        scratch_shapes=[pltpu.VMEM((G, BLK, 2 * width), f32), pltpu.VMEM((rows, width), bf16)],
        compiler_params=pltpu.CompilerParams(vmem_limit_bytes=20 << 20),
    )(
        random_blocks.transpose(2, 0, 1),
        global_blocks,
        queries,
        kv.reshape(nblk, BLK, 2 * width),
        grad,
        weight,
    )
    out, dk, dv = pl.pallas_call(
        reduce_kernel,
        name="reduce",
        out_shape=(
            jax.ShapeDtypeStruct((rows, cols), bf16),
            jax.ShapeDtypeStruct((rows, width), bf16),
            jax.ShapeDtypeStruct((rows, width), bf16),
        ),
        in_specs=[vmem, vmem],
        out_specs=(vmem, vmem, vmem),
        scratch_shapes=[
            pltpu.VMEM((cn, rows, 2 * width), bf16),
            pltpu.VMEM((2, cn, rows, 2 * width), bf16),
            pltpu.VMEM((ZN, rows, 2 * width), bf16),
            pltpu.VMEM((HN - 1, rows, cols), bf16),
            pltpu.VMEM((rows, 2 * width), f32),
            dma((cn * NP,)),
            dma((2 * cn * NP,)),
            dma((ZN * NP,)),
            dma((HN - 1,)),
            dma((HN - 1,)),
        ],
        compiler_params=pltpu.CompilerParams(
            collective_id=1, has_side_effects=True, vmem_limit_bytes=30 << 20
        ),
    )(part.reshape(cn, rows, 2 * width), outp)
    return (out, dq, dk, dv)


def solution(mesh):
    near = mesh.shape["ctx"] == YN * ZN and mesh.shape["head"] == HN
    placed = (
        P("ctx", "head"),
        P("ctx", "head"),
        P("ctx", "head"),
        P("ctx", "head"),
        P("head", None),
        P(),
        P(),
    )
    return jax.shard_map(
        near_body if near else body,
        mesh=mesh,
        in_specs=placed,
        out_specs=(P("ctx", "head"), P("ctx", "head"), P("ctx", "head"), P("ctx", "head")),
        check_vma=False,
    )
```

```python
import functools

import jax
import jax.numpy as jnp
from jax import lax
from jax.experimental import pallas as pl
from jax.experimental.pallas import tpu as pltpu
from jax.sharding import PartitionSpec as P

HD = 128
BLK = 64
R = 3
G = 2


def with_halo(cells, sides, width):
    for axis, dim in sides:
        count = lax.axis_size(axis)
        ends = count - 1
        head = lax.slice_in_dim(cells, 0, width, axis=dim)
        tail = lax.slice_in_dim(cells, cells.shape[dim] - width, cells.shape[dim], axis=dim)
        cells = jnp.concatenate(
            [
                lax.ppermute(tail, axis, [(i, (i + 1) % count) for i in range(ends)]),
                cells,
                lax.ppermute(head, axis, [((i + 1) % count, i) for i in range(ends)]),
            ],
            axis=dim,
        )
    return cells


def send_plan(request_table, shards, blocks, my_shard):
    requests = request_table.shape[1]
    owners = request_table // blocks
    within = request_table % blocks
    request_ids = jnp.arange(requests, dtype=jnp.int32)
    earlier = (owners[:, :, None] == owners[:, None, :]) & (
        request_ids[None, None, :] < request_ids[None, :, None]
    )
    ranking = jnp.sum(earlier.astype(jnp.int32), axis=2)
    capacity = (requests + shards - 2) // (shards - 1)
    slot_ids = jnp.arange(capacity, dtype=jnp.int32)
    owned = (owners == my_shard)[:, None, :] & (ranking[:, None, :] == slot_ids[None, :, None])
    tile_ids = (request_ids // (blocks * R))[None, :] * blocks + within
    send_tiles = jnp.sum(jnp.where(owned, tile_ids[:, None, :], 0), axis=2).reshape(-1)
    send_alive = jnp.any(owned, axis=2).reshape(-1)
    my_owners = lax.dynamic_index_in_dim(owners, my_shard, 0, keepdims=False)
    my_ranks = lax.dynamic_index_in_dim(ranking, my_shard, 0, keepdims=False)
    return (send_tiles, send_alive, my_owners * capacity + my_ranks)


def pick_tiles(pair_tiles, send_tiles, blocks):
    return pair_tiles[send_tiles % blocks, :, send_tiles // blocks, :]


def pair_products(row_tiles, window, global_pairs, fetched, low_edge, high_edge):
    nearby = jnp.einsum(
        "nqhd,nwbhd->nhqwb",
        row_tiles,
        window[..., low_edge:high_edge],
        preferred_element_type=jnp.float32,
    )
    distant = jnp.einsum(
        "nqhd,gbhd->nhqgb",
        row_tiles,
        global_pairs[..., low_edge:high_edge],
        preferred_element_type=jnp.float32,
    )
    chance = jnp.einsum(
        "nqhd,hnrbd->nhqrb",
        row_tiles,
        fetched[..., low_edge:high_edge],
        preferred_element_type=jnp.float32,
    )
    return jnp.concatenate([nearby, distant, chance], axis=3)


def collect_rows(mixing, window, global_pairs, fetched, low_edge, high_edge):
    nearby = jnp.einsum(
        "nhqwb,nwbhd->nqhd",
        mixing[:, :, :, :3],
        window[..., low_edge:high_edge],
        preferred_element_type=jnp.float32,
    )
    distant = jnp.einsum(
        "nhqgb,gbhd->nqhd",
        mixing[:, :, :, 3 : 3 + G],
        global_pairs[..., low_edge:high_edge],
        preferred_element_type=jnp.float32,
    )
    chance = jnp.einsum(
        "nhqrb,hnrbd->nqhd",
        mixing[:, :, :, 3 + G :],
        fetched[..., low_edge:high_edge],
        preferred_element_type=jnp.float32,
    )
    return nearby + distant + chance


def tile_terms(mixing, row_tiles):
    nearby = jnp.einsum(
        "nhqwb,nqhd->nwbhd", mixing[:, :, :, :3], row_tiles, preferred_element_type=jnp.float32
    )
    distant = jnp.einsum(
        "nhqgb,nqhd->gbhd",
        mixing[:, :, :, 3 : 3 + G],
        row_tiles,
        preferred_element_type=jnp.float32,
    )
    chance = jnp.einsum(
        "nhqrb,nqhd->hnrbd", mixing[:, :, :, 3 + G :], row_tiles, preferred_element_type=jnp.float32
    )
    return (nearby, distant, chance)


def body(queries, keys, values, output_grad, out_weight, random_blocks, global_blocks):
    shards = lax.axis_size("ctx")
    my_shard = lax.axis_index("ctx")
    head_group = lax.axis_index("head")
    tok_local, width_local = queries.shape
    head_dim = HD
    heads_local = width_local // head_dim
    blocks = tok_local // BLK
    scaling = head_dim ** (-0.5)
    query_tiles = queries.reshape(blocks, BLK, heads_local, head_dim)
    pair_tiles = jnp.concatenate(
        [
            keys.reshape(blocks, BLK, heads_local, head_dim),
            values.reshape(blocks, BLK, heads_local, head_dim),
        ],
        axis=3,
    )
    head_table = lax.dynamic_slice_in_dim(random_blocks, head_group * heads_local, heads_local, 0)
    request_table = (
        head_table.reshape(heads_local, shards, blocks, R)
        .transpose(1, 0, 2, 3)
        .reshape(shards, heads_local * blocks * R)
    )
    send_tiles, send_alive, receive_rows = send_plan(request_table, shards, blocks, my_shard)
    received = lax.all_to_all(
        pick_tiles(pair_tiles, send_tiles, blocks), "ctx", split_axis=0, concat_axis=0, tiled=True
    )
    fetched = received[receive_rows].reshape(heads_local, blocks, R, BLK, 2 * head_dim)
    padded = with_halo(pair_tiles.reshape(tok_local, 2 * width_local), (("ctx", 0),), BLK)
    padded = padded.reshape(blocks + 2, BLK, heads_local, 2 * head_dim)
    window = jnp.stack([padded[offset : offset + blocks] for offset in range(3)], axis=1)
    global_owner = global_blocks // blocks
    global_local = global_blocks % blocks
    picked = pair_tiles[global_local]
    holding = jnp.where(
        (global_owner == my_shard)[:, None, None, None], picked.astype(jnp.float32), 0.0
    )
    global_pairs = lax.psum(holding, "ctx").astype(jnp.bfloat16)
    first_block = my_shard * blocks
    window_ids = first_block + jnp.arange(blocks)[:, None] + jnp.arange(3)[None, :] - 1
    inside = (window_ids >= 0) & (window_ids < blocks * shards)
    alive_mask = jnp.concatenate([inside, jnp.ones((blocks, G + R), dtype=bool)], axis=1)[
        :, None, None, :, None
    ]
    logits = jnp.where(
        alive_mask,
        pair_products(query_tiles, window, global_pairs, fetched, 0, head_dim) * scaling,
        -jnp.inf,
    )
    row_max = jnp.max(logits, axis=(3, 4))
    log_total = row_max + jnp.log(jnp.sum(jnp.exp(logits - row_max[..., None, None]), axis=(3, 4)))
    weights_full = jnp.exp(logits - log_total[..., None, None])
    weights_low = weights_full.astype(jnp.bfloat16)
    attended = collect_rows(
        weights_low, window, global_pairs, fetched, head_dim, 2 * head_dim
    ).astype(jnp.bfloat16)
    attended_flat = attended.reshape(tok_local, width_local)
    partial_value = jnp.dot(attended_flat, out_weight, preferred_element_type=jnp.float32)
    output = lax.psum_scatter(partial_value, "head", scatter_dimension=1, tiled=True).astype(
        jnp.bfloat16
    )
    grad_sum = lax.dot_general(
        lax.all_gather(output_grad, "head", axis=1, tiled=True),
        out_weight,
        (((1,), (1,)), ((), ())),
        preferred_element_type=jnp.float32,
    )
    grad_tiles = grad_sum.astype(jnp.bfloat16).reshape(blocks, BLK, heads_local, head_dim)
    delta_rows = jnp.sum(
        grad_tiles.astype(jnp.float32) * attended.astype(jnp.float32), axis=3
    ).transpose(0, 2, 1)
    products = pair_products(grad_tiles, window, global_pairs, fetched, head_dim, 2 * head_dim)
    logit_grad = (weights_full * (products - delta_rows[..., None, None])).astype(jnp.bfloat16)
    query_grad = (
        (collect_rows(logit_grad, window, global_pairs, fetched, 0, head_dim) * scaling)
        .astype(jnp.bfloat16)
        .reshape(tok_local, width_local)
    )
    key_nearby, key_distant, key_chance = tile_terms(logit_grad, query_tiles)
    value_nearby, value_distant, value_chance = tile_terms(weights_low, grad_tiles)
    nearby_terms = jnp.concatenate([key_nearby * scaling, value_nearby], axis=4)
    framed = sum(
        (
            jnp.pad(nearby_terms[:, offset], ((offset, 2 - offset), (0, 0), (0, 0), (0, 0)))
            for offset in range(3)
        )
    )
    edge_rows = jnp.concatenate([framed[0], framed[blocks + 1]], axis=0).reshape(
        2 * BLK, 2 * width_local
    )
    arrived = with_halo(edge_rows.astype(jnp.bfloat16), (("ctx", 0),), BLK).astype(edge_rows.dtype)
    local_grad = framed[1 : blocks + 1]
    local_grad = local_grad.at[0].add(arrived[:BLK].reshape(BLK, heads_local, 2 * head_dim))
    local_grad = local_grad.at[blocks - 1].add(
        arrived[3 * BLK :].reshape(BLK, heads_local, 2 * head_dim)
    )
    distant_terms = jnp.concatenate([key_distant * scaling, value_distant], axis=3)
    summed = lax.psum(distant_terms, "ctx")
    selector = (
        (global_owner == my_shard)[:, None] & (global_local[:, None] == jnp.arange(blocks)[None, :])
    ).astype(jnp.float32)
    local_grad = local_grad + jnp.einsum(
        "gn,gbhd->nbhd", selector, summed, precision=lax.Precision.HIGHEST
    )
    chance_terms = (
        jnp.concatenate([key_chance * scaling, value_chance], axis=4)
        .astype(jnp.bfloat16)
        .reshape(-1, BLK, 2 * head_dim)
    )
    outgoing_grads = (
        jnp.zeros((send_tiles.shape[0], BLK, 2 * head_dim), jnp.bfloat16)
        .at[receive_rows]
        .set(chance_terms)
    )
    returned = lax.all_to_all(outgoing_grads, "ctx", split_axis=0, concat_axis=0, tiled=True)
    segment_ids = jnp.where(send_alive, send_tiles, heads_local * blocks)
    gathered = jax.ops.segment_sum(
        returned.astype(jnp.float32), segment_ids, num_segments=heads_local * blocks + 1
    )[: heads_local * blocks]
    local_grad = local_grad + gathered.reshape(heads_local, blocks, BLK, 2 * head_dim).transpose(
        1, 2, 0, 3
    )
    key_grad = local_grad[..., :head_dim].astype(jnp.bfloat16).reshape(tok_local, width_local)
    value_grad = local_grad[..., head_dim:].astype(jnp.bfloat16).reshape(tok_local, width_local)
    return (output, query_grad, key_grad, value_grad)


MESH = pl.DeviceIdType.MESH
YN = 2
ZN = 4
HN = 4
PARTS = ((0, 48, True), (48, 128, False), (128, 192, False), (192, 256, False))
NP = len(PARTS)


def greet(z, y, head):
    bar = pltpu.get_barrier_semaphore()

    def hello(target):
        pl.semaphore_signal(bar, inc=1, device_id=target, device_id_type=MESH)

    hello({"ctx": z * YN + (1 - y)})
    for d in range(1, HN):
        hello({"head": lax.rem(head + d, HN)})

    @pl.when(z > 0)
    def _():
        hello({"ctx": (z - 1) * YN + y})

    @pl.when(z < ZN - 1)
    def _():
        hello({"ctx": (z + 1) * YN + y})

    lower = jnp.where(z > 0, 1, 0)
    upper = jnp.where(z < ZN - 1, 1, 0)
    pl.semaphore_wait(bar, HN + lower + upper)


def gather_kernel(k_ref, v_ref, og_ref, w_hbm, kv_ref, do_ref, wbuf, ogbuf, oglocal, acc, wsem, lsem, ssem, rsem, hs, hr):
    me = lax.axis_index("ctx")
    head = lax.axis_index("head")
    z, y = me // YN, lax.rem(me, YN)
    width = k_ref.shape[1]
    cols = og_ref.shape[1]
    wcopy = pltpu.make_async_copy(w_hbm, wbuf, wsem)
    wcopy.start()
    kcopy = pltpu.make_async_copy(k_ref, kv_ref.at[me, :, pl.ds(0, width)], lsem.at[0])
    vcopy = pltpu.make_async_copy(v_ref, kv_ref.at[me, :, pl.ds(width, width)], lsem.at[1])
    ogcopy = pltpu.make_async_copy(og_ref, oglocal, lsem.at[2])
    kcopy.start()
    vcopy.start()
    ogcopy.start()
    greet(z, y, head)
    kcopy.wait()
    vcopy.wait()

    def copy(way, slot, p):
        lo, hi, _ = PARTS[p]
        at = kv_ref.at[slot, pl.ds(lo, hi - lo)]
        target = (z + 1) * YN + y if way == 0 else (z - 1) * YN + y if way == 1 else z * YN + (1 - y)
        return pltpu.make_async_remote_copy(
            src_ref=at,
            dst_ref=at,
            send_sem=ssem.at[(way * 8 + slot) * NP + p],
            recv_sem=rsem.at[slot * NP + p],
            device_id={"ctx": target},
            device_id_type=MESH,
        )

    def onward(way, slot, p, act):
        inside = z < ZN - 1 if way == 0 else z > 0

        @pl.when(inside)
        def _():
            act(copy(way, slot, p))

    def run(act, waiting):
        for p in range(NP):
            act(copy(2, me, p))
            onward(0, me, p, act)
            onward(1, me, p, act)
        if not waiting:
            send_heads()
            multiply(0)
        other = z * YN + (1 - y)
        for p in range(NP):
            if PARTS[p][2]:
                if not waiting:
                    copy(2, other, p).wait_recv()
                onward(0, other, p, act)
                onward(1, other, p, act)
        for t in range(1, ZN):
            for p in range(NP):
                for way in range(2):
                    zs = z - t if way == 0 else z + t

                    @pl.when((zs >= 0) & (zs < ZN))
                    def _():
                        slot = zs * YN + y
                        if not waiting:
                            copy(2, slot, p).wait_recv()
                        onward(way, slot, p, act)
                        if PARTS[p][2]:
                            over = zs * YN + (1 - y)
                            if not waiting:
                                copy(2, over, p).wait_recv()
                            onward(way, over, p, act)
                        else:
                            act(copy(2, slot, p))
            if not waiting:
                multiply(t)
        if not waiting:
            for zs in range(ZN):
                for p in range(NP):
                    if not PARTS[p][2]:
                        copy(2, zs * YN + (1 - y), p).wait_recv()

    order = (0, 1, 2, 3)

    def head_copy(d):
        return pltpu.make_async_remote_copy(
            src_ref=og_ref,
            dst_ref=ogbuf.at[d - 1],
            send_sem=hs.at[d - 1],
            recv_sem=hr.at[d - 1],
            device_id={"head": lax.rem(head + d, HN)},
            device_id_type=MESH,
        )

    def send_heads():
        for d in range(1, HN):
            head_copy(d).start()
        ogcopy.wait()
        wcopy.wait()

    def multiply(d):
        source = lax.rem(head - order[d] + HN, HN)
        if d:
            head_copy(d).wait_recv()
        shard = oglocal[...] if d == 0 else ogbuf[d - 1]
        weight = wbuf[:, pl.ds(pl.multiple_of(source * cols, cols), cols)]
        product = lax.dot_general(
            shard, weight, (((1,), (1,)), ((), ())), preferred_element_type=jnp.float32
        )
        if d == 0:
            acc[...] = product
        else:
            acc[...] += product

    run(lambda c: c.start(), False)
    do_ref[...] = acc[...].astype(jnp.bfloat16)
    run(lambda c: c.wait_send(), True)
    for d in range(1, HN):
        head_copy(d).wait_send()


def local_kernel(rb, gb, q_ref, kv_ref, do_ref, att_ref, dq_ref, dkv_ref, shared):
    me = lax.axis_index("ctx")
    group = lax.axis_index("head")
    nblk = kv_ref.shape[0]
    blocks = q_ref.shape[0] // BLK
    width = q_ref.shape[1]
    heads = width // HD
    scaling = HD ** (-0.5)
    dkv_ref[...] = jnp.zeros_like(dkv_ref)
    shared[...] = jnp.zeros_like(shared)
    nt = (((1,), (1,)), ((), ()))
    tn = (((0,), (0,)), ((), ()))
    nn = (((1,), (0,)), ((), ()))

    def dot(a, b, dims):
        return lax.dot_general(a, b, dims, preferred_element_type=jnp.float32)

    def step(n, carry):
        i = me * blocks + n
        rows = pl.ds(pl.multiple_of(n * BLK, BLK), BLK)
        column = lax.broadcasted_iota(jnp.int32, (BLK, 8 * BLK), 1)
        first_end = jnp.where(i == 0, BLK, 0)
        last_end = jnp.where(i == nblk - 1, 3 * BLK, 2 * BLK)
        dead = (column < first_end) | ((column >= 2 * BLK) & (column < last_end))
        late = []
        for h in range(heads):
            hc = slice(h * HD, (h + 1) * HD)
            vc = slice(width + h * HD, width + (h + 1) * HD)
            ids = [jnp.maximum(i - 1, 0), i, jnp.minimum(i + 1, nblk - 1), gb[0], gb[1]]
            ids = ids + [rb[r, group * heads + h, i] for r in range(R)]
            kg = jnp.concatenate([kv_ref[e, :, hc] for e in ids], axis=0)
            vg = jnp.concatenate([kv_ref[e, :, vc] for e in ids], axis=0)
            q = q_ref[rows, hc]
            do = do_ref[rows, hc]
            logits = jnp.where(dead, -jnp.inf, dot(q, kg, nt) * scaling)
            e = jnp.exp(logits - jnp.max(logits, axis=1, keepdims=True))
            weights = e * (1.0 / jnp.sum(e, axis=1, keepdims=True))
            low = weights.astype(jnp.bfloat16)
            att = dot(low, vg, nn).astype(jnp.bfloat16)
            att_ref[rows, hc] = att
            delta = jnp.sum(do.astype(jnp.float32) * att.astype(jnp.float32), axis=1, keepdims=True)
            lg = (weights * (dot(do, vg, nt) - delta)).astype(jnp.bfloat16)
            dq_ref[rows, hc] = (dot(lg, kg, nn) * scaling).astype(jnp.bfloat16)
            dk = dot(lg, q, tn) * scaling
            dv = dot(low, do, tn)
            late.append((hc, vc, ids, dk, dv))
        for hc, vc, ids, dk, dv in late:
            for g in range(G):
                shared[g, :, hc] += dk[(3 + g) * BLK : (4 + g) * BLK]
                shared[g, :, vc] += dv[(3 + g) * BLK : (4 + g) * BLK]
            for k in (0, 1, 2, 5, 6, 7):
                for at, term in ((hc, dk), (vc, dv)):
                    held = dkv_ref[ids[k], :, at].astype(jnp.float32)
                    held = held + term[k * BLK : (k + 1) * BLK]
                    dkv_ref[ids[k], :, at] = held.astype(jnp.bfloat16)
        return carry

    lax.fori_loop(0, blocks, step, 0)
    for g in range(G):
        held = dkv_ref[gb[g]].astype(jnp.float32)
        dkv_ref[gb[g]] = (held + shared[g]).astype(jnp.bfloat16)


def reduce_kernel(part_ref, att_ref, w_ref, out_ref, dk_ref, dv_ref, outp_ref, acc, rz, ry, ro, sums, ssem, zsem, ysem, hs, hr):
    me = lax.axis_index("ctx")
    head = lax.axis_index("head")
    z, y = me // YN, lax.rem(me, YN)
    width = dk_ref.shape[1]
    greet(z, y, head)

    def head_copy(d):
        target = lax.rem(head + d, HN)
        return pltpu.make_async_remote_copy(
            src_ref=outp_ref.at[target],
            dst_ref=ro.at[d - 1],
            send_sem=hs.at[d - 1],
            recv_sem=hr.at[d - 1],
            device_id={"head": target},
            device_id_type=MESH,
        )

    def span(p):
        return pl.ds(PARTS[p][0], PARTS[p][1] - PARTS[p][0])

    def zcopy(way, slot, p):
        return pltpu.make_async_remote_copy(
            src_ref=acc.at[slot, span(p)],
            dst_ref=rz.at[way, slot, span(p)],
            send_sem=ssem.at[slot * NP + p],
            recv_sem=zsem.at[(way * 8 + slot) * NP + p],
            device_id={"ctx": (jnp.minimum(z + 1, ZN - 1) if way == 0 else jnp.maximum(z - 1, 0)) * YN + y},
            device_id_type=MESH,
        )

    def ycopy(source, zd, p):
        return pltpu.make_async_remote_copy(
            src_ref=source.at[zd * YN + (1 - y), span(p)],
            dst_ref=ry.at[zd, span(p)],
            send_sem=ssem.at[(zd * YN + (1 - y)) * NP + p],
            recv_sem=ysem.at[zd * NP + p],
            device_id={"ctx": z * YN + (1 - y)},
            device_id_type=MESH,
        )

    def zadd(way, slot, p, total):
        zcopy(way, slot, p).wait_recv()
        return total + rz[way, slot, span(p)].astype(jnp.float32)

    def far(act):
        for t in range(ZN - 1, -1, -1):
            for way in range(2):
                if t == 0 and way:
                    continue
                zd = z + t if way == 0 else z - t

                @pl.when((zd >= 0) & (zd < ZN))
                def _():
                    act(zd, way, t)

    bulk = [p for p in range(NP) if not PARTS[p][2]]
    fast = [p for p in range(NP) if PARTS[p][2]]

    def start_y(zd, way, t):
        for p in bulk:
            ycopy(part_ref, zd, p).start()

    far(start_y)
    cols = out_ref.shape[1]
    for d in (2, 1, 3, 0):
        target = lax.rem(head + d, HN)
        outp_ref[target] = jnp.dot(
            att_ref[...],
            w_ref[:, pl.ds(pl.multiple_of(target * cols, cols), cols)],
            preferred_element_type=jnp.float32,
        ).astype(jnp.bfloat16)
        if d:
            head_copy(d).start()

    def pass_z(zd, way, t):
        if t == 0:
            return
        behind = z > 0 if way == 0 else z < ZN - 1
        for slot, p in [(zd * YN + (1 - y), p) for p in fast] + [(zd * YN + y, p) for p in range(NP)]:
            total = part_ref[slot, span(p)].astype(jnp.float32)
            if not PARTS[p][2]:
                ycopy(part_ref, zd, p).wait_recv()
                total = total + ry[zd, span(p)].astype(jnp.float32)
            acc[slot, span(p)] = total.astype(jnp.bfloat16)

            @pl.when(behind)
            def _():
                acc[slot, span(p)] = zadd(way, slot, p, acc[slot, span(p)].astype(jnp.float32)).astype(
                    jnp.bfloat16
                )

            zcopy(way, slot, p).start()

    far(pass_z)

    def settle(slot, p):
        sums[span(p)] = part_ref[slot, span(p)].astype(jnp.float32)

        @pl.when(z > 0)
        def _():
            sums[span(p)] = zadd(0, slot, p, sums[span(p)])

        @pl.when(z < ZN - 1)
        def _():
            sums[span(p)] = zadd(1, slot, p, sums[span(p)])

    other = z * YN + (1 - y)
    for p in fast:
        settle(other, p)
        acc[other, span(p)] = sums[span(p)].astype(jnp.bfloat16)
        ycopy(acc, z, p).start()
    total = outp_ref[head].astype(jnp.float32)
    for d in range(1, HN):
        head_copy(d).wait_recv()
        total = total + ro[d - 1].astype(jnp.float32)
    out_ref[...] = total.astype(jnp.bfloat16)
    for p in bulk + fast:
        settle(me, p)
        ycopy(part_ref if p in bulk else acc, z, p).wait_recv()
        grad = sums[span(p)] + ry[z, span(p)].astype(jnp.float32)
        dk_ref[span(p)] = grad[:, :width].astype(jnp.bfloat16)
        dv_ref[span(p)] = grad[:, width:].astype(jnp.bfloat16)

    def end_y(zd, way, t):
        for p in bulk:
            ycopy(part_ref, zd, p).wait_send()

    def end_z(zd, way, t):
        if t == 0:
            return
        for slot, p in [(zd * YN + (1 - y), p) for p in fast] + [(zd * YN + y, p) for p in range(NP)]:
            zcopy(way, slot, p).wait_send()

    far(end_y)
    far(end_z)
    for p in fast:
        ycopy(acc, z, p).wait_send()
    for d in range(1, HN):
        head_copy(d).wait_send()


def near_body(queries, keys, values, output_grad, out_weight, random_blocks, global_blocks):
    rows, width = queries.shape
    cols = output_grad.shape[1]
    cn = YN * ZN
    vmem = pl.BlockSpec(memory_space=pltpu.VMEM)
    smem = pl.BlockSpec(memory_space=pltpu.SMEM)
    hbm = pl.BlockSpec(memory_space=pltpu.HBM)
    bf16, f32 = jnp.bfloat16, jnp.float32
    dma = pltpu.SemaphoreType.DMA
    kv, grad, weight = pl.pallas_call(
        gather_kernel,
        name="gather",
        out_shape=(
            jax.ShapeDtypeStruct((cn, rows, 2 * width), bf16),
            jax.ShapeDtypeStruct((rows, width), bf16),
            jax.ShapeDtypeStruct(out_weight.shape, bf16),
        ),
        in_specs=[hbm, hbm, hbm, hbm],
        out_specs=(vmem, vmem, vmem),
        scratch_shapes=[
            pltpu.VMEM((HN - 1, rows, cols), bf16),
            pltpu.VMEM((rows, cols), bf16),
            pltpu.VMEM((rows, width), f32),
            dma,
            dma((3,)),
            dma((3 * cn * NP,)),
            dma((cn * NP,)),
            dma((HN - 1,)),
            dma((HN - 1,)),
        ],
        compiler_params=pltpu.CompilerParams(
            collective_id=0, has_side_effects=True, vmem_limit_bytes=16 << 20
        ),
    )(*(pltpu.with_memory_space_constraint(x, pltpu.HBM) for x in (keys, values, output_grad, out_weight)))
    nblk = cn * rows // BLK
    att, dq, part = pl.pallas_call(
        local_kernel,
        name="attention",
        out_shape=(
            jax.ShapeDtypeStruct((rows, width), bf16),
            jax.ShapeDtypeStruct((rows, width), bf16),
            jax.ShapeDtypeStruct((nblk, BLK, 2 * width), bf16),
        ),
        in_specs=[smem, smem, vmem, vmem, vmem],
        out_specs=(vmem, vmem, vmem),
        scratch_shapes=[pltpu.VMEM((G, BLK, 2 * width), f32)],
        compiler_params=pltpu.CompilerParams(vmem_limit_bytes=20 << 20),
    )(
        random_blocks.transpose(2, 0, 1),
        global_blocks,
        queries,
        kv.reshape(nblk, BLK, 2 * width),
        grad,
    )
    out, dk, dv = pl.pallas_call(
        reduce_kernel,
        name="reduce",
        out_shape=(
            jax.ShapeDtypeStruct((rows, cols), bf16),
            jax.ShapeDtypeStruct((rows, width), bf16),
            jax.ShapeDtypeStruct((rows, width), bf16),
        ),
        in_specs=[vmem, vmem, vmem],
        out_specs=(vmem, vmem, vmem),
        scratch_shapes=[
            pltpu.VMEM((HN, rows, cols), bf16),
            pltpu.VMEM((cn, rows, 2 * width), bf16),
            pltpu.VMEM((2, cn, rows, 2 * width), bf16),
            pltpu.VMEM((ZN, rows, 2 * width), bf16),
            pltpu.VMEM((HN - 1, rows, cols), bf16),
            pltpu.VMEM((rows, 2 * width), f32),
            dma((cn * NP,)),
            dma((2 * cn * NP,)),
            dma((ZN * NP,)),
            dma((HN - 1,)),
            dma((HN - 1,)),
        ],
        compiler_params=pltpu.CompilerParams(
            collective_id=1, has_side_effects=True, vmem_limit_bytes=30 << 20
        ),
    )(part.reshape(cn, rows, 2 * width), att, weight)
    return (out, dq, dk, dv)


def solution(mesh):
    near = mesh.shape["ctx"] == YN * ZN and mesh.shape["head"] == HN
    placed = (
        P("ctx", "head"),
        P("ctx", "head"),
        P("ctx", "head"),
        P("ctx", "head"),
        P("head", None),
        P(),
        P(),
    )
    return jax.shard_map(
        near_body if near else body,
        mesh=mesh,
        in_specs=placed,
        out_specs=(P("ctx", "head"), P("ctx", "head"), P("ctx", "head"), P("ctx", "head")),
        check_vma=False,
    )
```
